128 devices in a mesh: lon: 8 (over x_lo, y), lat: 16 (over z, x_hi, core).
Axes of the slice: x: 4 (x_hi: 2, x_lo: 2; x = x_hi * 2 + x_lo), y: 4, z: 4, core: 2. Of those that a mesh axis runs over, the one named last changes fastest.
Arguments:
- u_velocity: float32 [16, 2048, 4096], P(None, 'lat', 'lon'), may hold values from -6 to 6
- v_velocity: float32 [16, 2048, 4096], P(None, 'lat', 'lon'), may hold values from -6 to 6
- bottom_level: int32 [2048, 4096], P('lat', 'lon'), may hold values from 0 to 16
- zonal_scale: float32 [2048], P('lat'), may hold values from 0.5 to 2
- mixing: float32 [15], replicated, may hold values from 0.1 to 3
- brick_owner: int32 [128], replicated, may hold values from 0 to 127, each once
Outputs:
- bricks: bfloat16 [128, 128, 4, 16, 128], P(('lon', 'lat'))
The draws below stay inside these ranges and needn't reach their ends.
Inputs may be any that keep to these rules, and one draw needn't show every extreme that they name: `brick_owner`: a permutation of the device numbers 0 to 127.
All inputs are finite; a program needn't handle non-finite values.
Results may differ from the reference program's by a relative error of at most 0.001.
Values may be sent and summed in bfloat16 or wider, within the bound.
A program may use at most 128 MiB of HBM per device.

```python
import math
import jax
import jax.numpy as jnp
from jax import lax

LEV = 16
LAT_DEV = 128
NY = 2048
NX = 4096
ROW_GROUPS = 8
BRICK_LEV = 4
BRICK_ROWS = 16
BRICK_COLS = 128
N_LON = 8
N_LAT = 16


def set_ends(values, rng, smallest, largest):
    spot = [jax.random.randint(jax.random.fold_in(rng, axis), (), 0, length) for axis, length in enumerate(values.shape)]
    widest = values.shape.index(max(values.shape))
    beside = spot[:widest] + [(spot[widest] + 1) % values.shape[widest]] + spot[widest + 1:]
    return values.at[tuple(spot)].set(smallest).at[tuple(beside)].set(largest)


def block_scale(key, extent, pieces, smallest, top_value):
    gain = 1.0
    for position, shards_of in pieces:
        heights = jax.random.uniform(jax.random.fold_in(jax.random.fold_in(key, 6), position), (shards_of,), jnp.float32, smallest / len(pieces), top_value / len(pieces))
        gain = gain * jnp.repeat(jnp.exp(heights), extent[position] // shards_of).reshape((-1,) + (1,) * (len(extent) - 1 - position))
    return gain


def centred(stream_key, dims, spread, reach, pieces=(), held_as=jnp.bfloat16):
    level = block_scale(stream_key, dims, pieces, -0.22, 0.18) if pieces else 1.0
    drawn = jax.random.normal(stream_key, dims, jnp.float32) * spread * level
    return jnp.minimum(jnp.maximum(drawn, -reach), reach).astype(held_as)


def setup_inputs(seed: int = 0) -> dict:
    arg_keys = jax.random.split(jax.random.key(seed), 7)
    u_velocity = centred(arg_keys[0], (LEV, NY, NX), 1.0, 6.0, ((1, 16), (2, 8)), jnp.float32)
    v_velocity = centred(arg_keys[1], (LEV, NY, NX), 1.0, 6.0, ((1, 16), (2, 8)), jnp.float32)
    bottom_level = set_ends(jax.random.randint(arg_keys[2], (NY, NX), 0, LEV + 1), jax.random.fold_in(arg_keys[2], 1), 0, LEV).astype(jnp.int32)
    zonal_scale = jnp.clip(jnp.exp(math.log(2.0) - 1.3862944 * jax.random.uniform(arg_keys[3], (NY,), jnp.float32) ** block_scale(arg_keys[3], (NY,), ((0, 16),), -0.2, 0.2)), 0.5, 2.0)
    mixing = jnp.clip(jnp.exp(jax.random.uniform(arg_keys[4], (LEV - 1,), jnp.float32, math.log(0.1), math.log(3.0))), 0.1, 3.0)
    brick_owner = jax.random.permutation(arg_keys[5], N_LON * N_LAT).astype(jnp.int32)
    return {"u_velocity": u_velocity, "v_velocity": v_velocity, "bottom_level": bottom_level, "zonal_scale": zonal_scale, "mixing": mixing, "brick_owner": brick_owner}


def fourth(first, second, third, fourth_term):
    return ((first - 8.0 * second) + 8.0 * third - fourth_term) * (1.0 / 12.0)


def okubo_weiss(zonal_u, zonal_v, north_u, north_v, scale, sea_mask):
    row_scale = scale[:, None]
    du_dx = fourth(zonal_u[..., :-4], zonal_u[..., 1:-3], zonal_u[..., 3:-1], zonal_u[..., 4:]) * row_scale
    dv_dx = fourth(zonal_v[..., :-4], zonal_v[..., 1:-3], zonal_v[..., 3:-1], zonal_v[..., 4:]) * row_scale
    du_dy = fourth(north_u[..., :-4, :], north_u[..., 1:-3, :], north_u[..., 3:-1, :], north_u[..., 4:, :])
    dv_dy = fourth(north_v[..., :-4, :], north_v[..., 1:-3, :], north_v[..., 3:-1, :], north_v[..., 4:, :])
    strain_normal = du_dx - dv_dy
    strain_shear = dv_dx + du_dy
    vorticity = dv_dx - du_dy
    return sea_mask * (strain_normal * strain_normal + strain_shear * strain_shear - vorticity * vorticity)


def smooth(field, mixing):
    levels = field.shape[0]
    subdiag = [None] + [-mixing[k - 1] for k in range(1, levels)]
    superdiag = [-mixing[k] for k in range(levels - 1)] + [None]
    diagonal = []
    for k in range(levels):
        center = jnp.float32(1.0)
        if k > 0:
            center = center + mixing[k - 1]
        if k < levels - 1:
            center = center + mixing[k]
        diagonal.append(center)
    ratios = []
    forward = []
    for k in range(levels):
        if k == 0:
            divisor = diagonal[0]
            current = field[0] / divisor
        else:
            divisor = diagonal[k] - subdiag[k] * ratios[k - 1]
            current = (field[k] - subdiag[k] * forward[k - 1]) / divisor
        ratios.append(superdiag[k] / divisor if k < levels - 1 else None)
        forward.append(current)
    result = [None] * levels
    result[levels - 1] = forward[levels - 1]
    for k in range(levels - 2, -1, -1):
        result[k] = forward[k] - ratios[k] * result[k + 1]
    return jnp.stack(result)


def reference(u_velocity, v_velocity, bottom_level, zonal_scale, mixing, brick_owner):
    levels, total_rows, total_cols = u_velocity.shape
    sea_full = (jnp.arange(levels, dtype=jnp.int32)[:, None, None] < bottom_level[None]).astype(jnp.float32)

    def extend(field):
        masked = field * sea_full
        ghost = -masked[:, total_rows - 2:, :][:, ::-1, ::-1]
        south = jnp.zeros((levels, 2, total_cols), jnp.float32)
        return jnp.concatenate([south, masked, ghost], axis=1)

    padded_u = extend(u_velocity)
    padded_v = extend(v_velocity)

    def band(index):
        start = index * LAT_DEV
        north_u = lax.dynamic_slice_in_dim(padded_u, start, LAT_DEV + 4, 1)
        north_v = lax.dynamic_slice_in_dim(padded_v, start, LAT_DEV + 4, 1)
        center_u = north_u[:, 2:LAT_DEV + 2, :]
        center_v = north_v[:, 2:LAT_DEV + 2, :]
        zonal_u = jnp.concatenate([center_u[..., -2:], center_u, center_u[..., :2]], axis=-1)
        zonal_v = jnp.concatenate([center_v[..., -2:], center_v, center_v[..., :2]], axis=-1)
        scale = lax.dynamic_slice_in_dim(zonal_scale, start, LAT_DEV, 0)
        sea_band = lax.dynamic_slice_in_dim(sea_full, start, LAT_DEV, 1)
        okubo = okubo_weiss(zonal_u, zonal_v, north_u, north_v, scale, sea_band)
        return smooth(okubo, mixing).astype(jnp.bfloat16)

    bands = lax.map(band, jnp.arange(N_LAT, dtype=jnp.int32))
    devices = N_LON * N_LAT
    tiles = bands.reshape(N_LAT, 4, BRICK_LEV, ROW_GROUPS, BRICK_ROWS, N_LON, 4, BRICK_COLS)
    tiles = jnp.transpose(tiles, (5, 0, 1, 3, 6, 2, 4, 7))
    tiles = tiles.reshape(devices, devices, BRICK_LEV, BRICK_ROWS, BRICK_COLS)
    slots = jnp.arange(devices, dtype=jnp.int32)
    inverse = jnp.sum(jnp.where(brick_owner[None, :] == slots[:, None], slots[None, :], 0), axis=1).astype(jnp.int32)
    chosen = jnp.take(tiles, inverse, axis=1)
    return jnp.transpose(chosen, (1, 0, 2, 3, 4))
```

```python
import jax
import jax.numpy as jnp
from jax import lax
from jax.experimental import pallas as pl
from jax.experimental.pallas import tpu as pltpu
from jax.sharding import PartitionSpec as P

MESH = pl.DeviceIdType.MESH
LEV, ROWS, TILES, LANES = 16, 128, 4, 128
N_LON, N_LAT = 8, 16
DEVICES = N_LON * N_LAT
COLUMNS = 32
GROUP = 4


def target(lon, lat, step):
    off = (step * 101) % DEVICES
    x = (lat % 4 // 2 * 2 + lon // 4 + off % 4) % 4
    y = (lon % 4 + off // 4 % 4) % 4
    z = (lat // 4 + off // 16 % 4) % 4
    core = (lat % 2 + off // 64) % 2
    return x % 2 * 4 + y, z * 4 + x // 2 * 2 + core


def plan(brick_owner):
    lon, lat = lax.axis_index("lon"), lax.axis_index("lat")
    steps = jnp.arange(DEVICES, dtype=jnp.int32)
    to_lon, to_lat = target(lon, lat, steps + 1)
    dest = to_lon * N_LAT + to_lat
    place = jnp.sum(jnp.where(brick_owner[None, :] == dest[:, None], steps[None, :], 0), axis=1)
    return place


def kernel(
    u_hbm, v_hbm, bottom_hbm, scale_ref, mixing_ref, plan_ref, out_ref,
    ub, vb, bottom, scale, coef, bricks, outbox, rows_out, rows_in, cols_out, cols_in,
    load_sem, bottom_sem, halo_send, halo_recv, own_sem, send_sem, recv_sem, ready,
):
    lon, lat = lax.axis_index("lon"), lax.axis_index("lat")
    me = lon * N_LAT + lat
    barrier = pltpu.get_barrier_semaphore()

    def signal(sem, to):
        pl.semaphore_signal(sem, inc=1, device_id=to, device_id_type=MESH)

    for k in range(1, N_LAT):
        signal(barrier, (lon, (lat + k) % N_LAT))
    for k in range(1, N_LON):
        signal(barrier, ((lon + k) % N_LON, lat))

    loads = []
    for t in range(TILES):
        cut = pl.ds(t * LANES, LANES)
        c = pltpu.make_async_copy(bottom_hbm.at[:, cut], bottom.at[t], bottom_sem.at[t])
        c.start()
        loads.append(c)
    for g in range(LEV // GROUP):
        for t in range(TILES):
            cut = pl.ds(t * LANES, LANES)
            levels = pl.ds(g * GROUP, GROUP)
            for f, (src, dst) in enumerate(((u_hbm, ub), (v_hbm, vb))):
                c = pltpu.make_async_copy(
                    src.at[levels, :, cut],
                    dst.at[levels, t + 1, pl.ds(8, ROWS), :],
                    load_sem.at[g, t, f],
                )
                c.start()
                loads.append(c)

    scale[...] = jnp.broadcast_to(scale_ref[...], (ROWS, LANES)).T
    one = jnp.ones((8, LANES), jnp.float32)
    ratio = None
    for k in range(LEV):
        above = mixing_ref[k - 1] * one if k > 0 else None
        below = mixing_ref[k] * one if k < LEV - 1 else None
        pivot = one
        if k > 0:
            pivot = pivot + above
        if k < LEV - 1:
            pivot = pivot + below
        if k > 0:
            pivot = pivot - above * ratio
        inverse = 1.0 / pivot
        coef[k] = inverse * (1.0 / 144.0)
        if k > 0:
            coef[LEV + k] = above * inverse
        if k < LEV - 1:
            ratio = below * inverse
            coef[2 * LEV + k] = ratio

    sub = lax.broadcasted_iota(jnp.int32, (8, LANES), 0)
    lane = lax.broadcasted_iota(jnp.int32, (64, LANES), 1)

    for c in loads[:TILES]:
        c.wait()
    west = jnp.zeros((64, LANES), jnp.float32)
    east = jnp.zeros((64, LANES), jnp.float32)
    for g in range(LEV // GROUP):
        for c in loads[TILES + g * 2 * TILES : TILES + (g + 1) * 2 * TILES]:
            c.wait()

        def mask_pair(n, carry):
            west, east = carry
            for j in range(2):
                k = g * GROUP + 2 * n + j
                for t in range(TILES):
                    sea = bottom[t] > k
                    for buf in (ub, vb):
                        now = buf[k, t + 1, pl.ds(8, ROWS), :]
                        buf[k, t + 1, pl.ds(8, ROWS), :] = jnp.where(sea, now, 0.0)
                for f, buf in enumerate((ub, vb)):
                    at = 4 * k + 2 * f
                    for half in range(2):
                        first = buf[k, 1, pl.ds(8 + 64 * half, 64), :]
                        last = buf[k, TILES, pl.ds(8 + 64 * half, 64), :]
                        spot = at + 64 * half
                        here = (lane >= spot) & (lane < spot + 2)
                        west = jnp.where(here, pltpu.roll(first, spot, 1), west)
                        east = jnp.where(here, pltpu.roll(last, (spot + 2) % LANES, 1), east)
            k = g * GROUP + 2 * n
            pair = k // 2
            for t in range(TILES):
                top = [b[k + j, t + 1, pl.ds(ROWS, 8), :] for j in range(2) for b in (ub, vb)]
                low = [b[k + j, t + 1, pl.ds(8, 8), :] for j in range(2) for b in (ub, vb)]
                top = [pltpu.roll(x, s, 0) if s else x for x, s in zip(top, (2, 4, 6, 0))]
                low = [pltpu.roll(x, s, 0) if s else x for x, s in zip(low, (0, 2, 4, 6))]
                for side, q in ((0, top), (1, low)):
                    rows_out[side, pair, t] = jnp.where(
                        sub < 4, jnp.where(sub < 2, q[0], q[1]), jnp.where(sub < 6, q[2], q[3])
                    )
            return west, east

        west, east = lax.fori_loop(0, GROUP // 2, mask_pair, (west, east))
    cols_out[0] = west
    cols_out[1] = east

    pl.semaphore_wait(barrier, N_LAT - 1 + N_LON - 1)
    for k in range(1, N_LON):
        signal(ready, ((lon + k) % N_LON, lat))

    def column_copy(side):
        to = (lon + (N_LON - 1 if side == 0 else 1)) % N_LON
        return pltpu.make_async_remote_copy(
            cols_out.at[side], cols_in.at[side], halo_send.at[side], halo_recv.at[side],
            device_id=(to, lat), device_id_type=MESH,
        )

    def row_copy(src, dst, sem, to):
        return pltpu.make_async_remote_copy(
            rows_out.at[src], rows_in.at[dst], halo_send.at[sem], halo_recv.at[2 + dst],
            device_id=to, device_id_type=MESH,
        )

    top_tile = lat == N_LAT - 1
    north = row_copy(0, 0, 2, (lon, (lat + 1) % N_LAT))
    fold = row_copy(0, 1, 2, (N_LON - 1 - lon, lat))
    south = row_copy(1, 1, 3, (lon, (lat + N_LAT - 1) % N_LAT))

    @pl.when(top_tile)
    def _():
        fold.start()

    @pl.when(jnp.logical_not(top_tile))
    def _():
        north.start()

    @pl.when(lat > 0)
    def _():
        south.start()

    for side in range(2):
        column_copy(side).start()

    @pl.when(lat == 0)
    def _():
        rows_in[0] = jnp.zeros(rows_in.shape[1:], jnp.float32)

    for side in range(2):
        column_copy(side).wait_recv()

    def spread_columns(k, _):
        for f, buf in enumerate((ub, vb)):
            for half in range(2):
                spot = 4 * k + 2 * f + 64 * half
                rows = pl.ds(8 + 64 * half, 64)
                buf[k, 0, rows, :] = pltpu.roll(cols_in[1], (126 - spot + LANES) % LANES, 1)
                buf[k, TILES + 1, rows, :] = pltpu.roll(cols_in[0], (LANES - spot) % LANES, 1)
        return _

    lax.fori_loop(0, LEV, spread_columns, 0)

    @pl.when(lat > 0)
    def _():
        north.wait_recv()

    south.wait_recv()

    @pl.when(top_tile)
    def _():
        lanes = lax.broadcasted_iota(jnp.int32, (8, LANES), 1)

        def turn(pair, _):
            old = [rows_in[1, pair, t] for t in range(TILES)]
            for t in range(TILES):
                x = old[TILES - 1 - t]
                x = jnp.where(sub % 2 == 0, pltpu.roll(x, 7, 0), pltpu.roll(x, 1, 0))
                rows_in[1, pair, t] = -jnp.take_along_axis(x, LANES - 1 - lanes, axis=1)
            return _

        lax.fori_loop(0, LEV // 2, turn, 0)

    def spread_rows(pair, _):
        for t in range(TILES):
            for side, shifts, rows in ((0, (6, 4, 2, 0), pl.ds(0, 8)), (1, (0, 6, 4, 2), pl.ds(ROWS + 8, 8))):
                x = rows_in[side, pair, t]
                for n, s in enumerate(shifts):
                    buf = (ub, vb)[n % 2]
                    buf[2 * pair + n // 2, t + 1, rows, :] = pltpu.roll(x, s, 0) if s else x
        return _

    lax.fori_loop(0, LEV // 2, spread_rows, 0)

    lanes = lax.broadcasted_iota(jnp.int32, (8, LANES), 1)

    def slopes(buf, k, c, row):
        here = buf[k, c + 1, pl.ds(row + 8, 8), :]
        left = buf[k, c, pl.ds(row + 8, 8), :]
        right = buf[k, c + 2, pl.ds(row + 8, 8), :]

        def beside(s):
            if s < 0:
                return pltpu.roll(jnp.where(lanes < LANES + s, here, left), -s, 1)
            return pltpu.roll(jnp.where(lanes >= s, here, right), LANES - s, 1)

        def above(s):
            return buf[k, c + 1, pl.ds(row + 8 + s, 8), :]

        def slope(at):
            return (at(-2) - at(2)) + 8.0 * (at(1) - at(-1))

        return slope(beside), slope(above)

    def compute(j):
        c = j % TILES
        row0 = pl.multiple_of(j // TILES * 16, 16)
        halves = []
        for h in range(2):
            row = row0 + 8 * h
            depth = bottom[c, pl.ds(row, 8), :]
            wide = scale[pl.ds(row, 8), :]
            wide4 = 4.0 * wide
            state = []
            for k in range(LEV):
                ux, uy = slopes(ub, k, c, row)
                vx, vy = slopes(vb, k, c, row)
                strain = ux * wide - vy
                okubo = strain * strain + (vx * wide4) * uy
                value = okubo * jnp.where(depth > k, coef[k], 0.0)
                if k > 0:
                    value = value + coef[LEV + k] * state[k - 1]
                state.append(value)
            for k in range(LEV - 2, -1, -1):
                state[k] = state[k] + coef[2 * LEV + k] * state[k + 1]
            halves.append(state)
        for k in range(LEV):
            both = jnp.concatenate([halves[0][k], halves[1][k]], axis=0)
            bricks[k // 4 * COLUMNS + j, k % 4] = both.astype(jnp.bfloat16)

    def send(step):
        to_lon, to_lat = target(lon, lat, step + 1)
        outbox[step] = bricks[plan_ref[step]]
        pltpu.make_async_remote_copy(
            outbox.at[step], out_ref.at[me], send_sem, recv_sem,
            device_id=(to_lon, to_lat), device_id_type=MESH,
        ).start()

    compute(0)
    pl.semaphore_wait(ready, N_LON - 1)

    def more(j, _):
        compute(j)
        return _

    lax.fori_loop(1, COLUMNS, more, 0)

    def rest(step, _):
        send(step)
        return _

    lax.fori_loop(0, DEVICES - 1, rest, 0)
    out_ref[me] = bricks[plan_ref[DEVICES - 1]]

    column_copy(0).wait_send()
    column_copy(1).wait_send()
    north.wait_send()

    @pl.when(lat > 0)
    def _():
        south.wait_send()

    whole = pltpu.make_async_remote_copy(
        outbox.at[pl.ds(0, DEVICES - 1)], out_ref.at[pl.ds(0, DEVICES - 1)], send_sem, recv_sem,
        device_id=(lon, lat), device_id_type=MESH,
    )
    whole.wait_send()
    whole.wait_recv()


def body(u_velocity, v_velocity, bottom_level, zonal_scale, mixing, brick_owner):
    brick = (DEVICES, 4, 16, LANES)
    dma = pltpu.SemaphoreType.DMA
    vmem, smem, hbm = (
        pl.BlockSpec(memory_space=pltpu.VMEM),
        pl.BlockSpec(memory_space=pltpu.SMEM),
        pl.BlockSpec(memory_space=pltpu.HBM),
    )
    out = pl.pallas_call(
        kernel,
        out_shape=pltpu.VMEM(brick, jnp.bfloat16),
        in_specs=[hbm, hbm, hbm, vmem, smem, smem],
        out_specs=vmem,
        scratch_shapes=[
            pltpu.VMEM((LEV, TILES + 2, ROWS + 16, LANES), jnp.float32),
            pltpu.VMEM((LEV, TILES + 2, ROWS + 16, LANES), jnp.float32),
            pltpu.VMEM((TILES, ROWS, LANES), jnp.int32),
            pltpu.VMEM((ROWS, LANES), jnp.float32),
            pltpu.VMEM((3 * LEV, 8, LANES), jnp.float32),
            pltpu.VMEM(brick, jnp.bfloat16),
            pltpu.VMEM(brick, jnp.bfloat16),
            pltpu.VMEM((2, LEV // 2, TILES, 8, LANES), jnp.float32),
            pltpu.VMEM((2, LEV // 2, TILES, 8, LANES), jnp.float32),
            pltpu.VMEM((2, 64, LANES), jnp.float32),
            pltpu.VMEM((2, 64, LANES), jnp.float32),
            dma((LEV // GROUP, TILES, 2)),
            dma((TILES,)),
            dma((4,)),
            dma((4,)),
            dma,
            dma,
            dma,
            pltpu.SemaphoreType.REGULAR,
        ],
        compiler_params=pltpu.CompilerParams(
            collective_id=0, has_side_effects=True, vmem_limit_bytes=48 << 20
        ),
    )(u_velocity, v_velocity, bottom_level, zonal_scale[None], mixing, plan(brick_owner))
    return out[None]


def solution(mesh):
    placed = (P(None, "lat", "lon"), P(None, "lat", "lon"), P("lat", "lon"), P("lat"), P(), P())
    return jax.shard_map(
        body,
        mesh=mesh,
        in_specs=placed,
        out_specs=P(("lon", "lat"), None, None, None, None),
        check_vma=False,
    )
```

```python
import jax
import jax.numpy as jnp
from jax import lax
from jax.experimental import pallas as pl
from jax.experimental.pallas import tpu as pltpu
from jax.sharding import PartitionSpec as P

MESH = pl.DeviceIdType.MESH
LEV, ROWS, TILES, LANES = 16, 128, 4, 128
N_LON, N_LAT = 8, 16
DEVICES = N_LON * N_LAT
COLUMNS = 32
PARTS = 3
GROUP = 4


def target(lon, lat, step):
    off = (step * 101) % DEVICES
    x = (lat % 4 // 2 * 2 + lon // 4 + off % 4) % 4
    y = (lon % 4 + off // 4 % 4) % 4
    z = (lat // 4 + off // 16 % 4) % 4
    core = (lat % 2 + off // 64) % 2
    return x % 2 * 4 + y, z * 4 + x // 2 * 2 + core


def plan(brick_owner):
    lon, lat = lax.axis_index("lon"), lax.axis_index("lat")
    steps = jnp.arange(DEVICES, dtype=jnp.int32)
    to_lon, to_lat = target(lon, lat, steps + 1)
    dest = to_lon * N_LAT + to_lat
    place = jnp.sum(jnp.where(brick_owner[None, :] == dest[:, None], steps[None, :], 0), axis=1)
    column = place % COLUMNS
    columns = jnp.arange(COLUMNS, dtype=jnp.int32)
    hit = column[None, :] == columns[:, None]
    need = jnp.min(jnp.where(hit, steps[None, :], DEVICES), axis=1)
    slot = jnp.sum((need[None, :] < need[:, None]).astype(jnp.int32), axis=1)
    order = jnp.sum(jnp.where(slot[None, :] == columns[:, None], columns[None, :], 0), axis=1)
    source = place // COLUMNS * COLUMNS + jnp.sum(jnp.where(hit, slot[:, None], 0), axis=0)
    return jnp.concatenate([order % TILES, order // TILES, source])


def split(x):
    parts = []
    for _ in range(PARTS - 1):
        part = x.astype(jnp.bfloat16)
        parts.append(part)
        x = x - part.astype(jnp.float32)
    return (*parts, x.astype(jnp.bfloat16))


def band_matrix():
    shape = (2 * LANES, LANES)
    row = lax.broadcasted_iota(jnp.int32, shape, 0)
    source = jnp.where(row < LANES, row, jnp.where(row < LANES + 64, row, row - 2 * LANES))
    gap = source - lax.broadcasted_iota(jnp.int32, shape, 1)
    weight = jnp.zeros(shape, jnp.float32)
    for at, w in ((-2, 1.0), (-1, -8.0), (1, 8.0), (2, -1.0)):
        weight = jnp.where(gap == at, w, weight)
    return weight.astype(jnp.bfloat16)


def kernel(
    u_hbm, v_hbm, bottom_hbm, scale_ref, mixing_ref, plan_ref, out_ref,
    ub, vb, parts, band, dx, bottom, scale, coef, bricks, outbox, rows_out, rows_in, cols_out, cols_in,
    load_sem, bottom_sem, halo_send, halo_recv, own_sem, send_sem, recv_sem, ready,
):
    lon, lat = lax.axis_index("lon"), lax.axis_index("lat")
    me = lon * N_LAT + lat
    barrier = pltpu.get_barrier_semaphore()

    def signal(sem, to):
        pl.semaphore_signal(sem, inc=1, device_id=to, device_id_type=MESH)

    for k in range(1, N_LAT):
        signal(barrier, (lon, (lat + k) % N_LAT))
    for k in range(1, N_LON):
        signal(barrier, ((lon + k) % N_LON, lat))

    loads = []
    for t in range(TILES):
        cut = pl.ds(t * LANES, LANES)
        c = pltpu.make_async_copy(bottom_hbm.at[:, :, cut], bottom.at[t], bottom_sem.at[t])
        c.start()
        loads.append(c)
    for g in range(LEV // GROUP):
        for t in range(TILES):
            cut = pl.ds(t * LANES, LANES)
            levels = pl.ds(g * GROUP, GROUP)
            for f, (src, dst) in enumerate(((u_hbm, ub), (v_hbm, vb))):
                c = pltpu.make_async_copy(
                    src.at[levels, :, :, cut],
                    dst.at[levels, t, pl.ds(1, ROWS // 8)],
                    load_sem.at[g, t, f],
                )
                c.start()
                loads.append(c)

    scale[...] = jnp.broadcast_to(scale_ref[...], (ROWS, LANES)).T.reshape(ROWS // 8, 8, LANES)
    band[...] = band_matrix()
    one = jnp.ones((8, LANES), jnp.float32)
    ratio = None
    for k in range(LEV):
        above = mixing_ref[k - 1] * one if k > 0 else None
        below = mixing_ref[k] * one if k < LEV - 1 else None
        pivot = one
        if k > 0:
            pivot = pivot + above
        if k < LEV - 1:
            pivot = pivot + below
        if k > 0:
            pivot = pivot - above * ratio
        inverse = 1.0 / pivot
        coef[k] = inverse * (1.0 / 144.0)
        if k > 0:
            coef[LEV + k] = above * inverse
        if k < LEV - 1:
            ratio = below * inverse
            coef[2 * LEV + k] = ratio

    sub = lax.broadcasted_iota(jnp.int32, (8, LANES), 0)
    lane = lax.broadcasted_iota(jnp.int32, (64, LANES), 1)

    for c in loads[:TILES]:
        c.wait()
    west = jnp.zeros((64, LANES), jnp.float32)
    east = jnp.zeros((64, LANES), jnp.float32)
    for g in range(LEV // GROUP):
        for c in loads[TILES + g * 2 * TILES : TILES + (g + 1) * 2 * TILES]:
            c.wait()

        def mask_pair(n, carry):
            west, east = carry
            for j in range(2):
                k = g * GROUP + 2 * n + j
                for t in range(TILES):
                    sea = bottom[t] > k
                    for f, buf in enumerate((ub, vb)):
                        now = jnp.where(sea, buf[k, t, pl.ds(1, ROWS // 8)], 0.0)
                        buf[k, t, pl.ds(1, ROWS // 8)] = now
                        for p, part in enumerate(split(now.reshape(ROWS, LANES))):
                            parts[f, p, k, t + 1] = part.reshape(ROWS // 16, 16, LANES)
                for f, buf in enumerate((ub, vb)):
                    at = 4 * k + 2 * f
                    for half in range(2):
                        first = buf[k, 0, pl.ds(1 + 8 * half, 8)].reshape(64, LANES)
                        last = buf[k, TILES - 1, pl.ds(1 + 8 * half, 8)].reshape(64, LANES)
                        spot = at + 64 * half
                        here = (lane >= spot) & (lane < spot + 2)
                        west = jnp.where(here, pltpu.roll(first, spot, 1), west)
                        east = jnp.where(here, pltpu.roll(last, (spot + 2) % LANES, 1), east)
            k = g * GROUP + 2 * n
            pair = k // 2
            for t in range(TILES):
                top = [b[k + j, t, ROWS // 8] for j in range(2) for b in (ub, vb)]
                low = [b[k + j, t, 1] for j in range(2) for b in (ub, vb)]
                top = [pltpu.roll(x, s, 0) if s else x for x, s in zip(top, (2, 4, 6, 0))]
                low = [pltpu.roll(x, s, 0) if s else x for x, s in zip(low, (0, 2, 4, 6))]
                for side, q in ((0, top), (1, low)):
                    rows_out[side, pair, t] = jnp.where(
                        sub < 4, jnp.where(sub < 2, q[0], q[1]), jnp.where(sub < 6, q[2], q[3])
                    )
            return west, east

        west, east = lax.fori_loop(0, GROUP // 2, mask_pair, (west, east))
    cols_out[0] = west
    cols_out[1] = east

    pl.semaphore_wait(barrier, N_LAT - 1 + N_LON - 1)
    for k in range(1, N_LON):
        signal(ready, ((lon + k) % N_LON, lat))

    def column_copy(side):
        to = (lon + (N_LON - 1 if side == 0 else 1)) % N_LON
        return pltpu.make_async_remote_copy(
            cols_out.at[side], cols_in.at[side], halo_send.at[side], halo_recv.at[side],
            device_id=(to, lat), device_id_type=MESH,
        )

    def row_copy(src, dst, sem, to):
        return pltpu.make_async_remote_copy(
            rows_out.at[src], rows_in.at[dst], halo_send.at[sem], halo_recv.at[2 + dst],
            device_id=to, device_id_type=MESH,
        )

    top_tile = lat == N_LAT - 1
    north = row_copy(0, 0, 2, (lon, (lat + 1) % N_LAT))
    fold = row_copy(0, 1, 2, (N_LON - 1 - lon, lat))
    south = row_copy(1, 1, 3, (lon, (lat + N_LAT - 1) % N_LAT))

    @pl.when(top_tile)
    def _():
        fold.start()

    @pl.when(jnp.logical_not(top_tile))
    def _():
        north.start()

    @pl.when(lat > 0)
    def _():
        south.start()

    for side in range(2):
        column_copy(side).start()

    @pl.when(lat == 0)
    def _():
        rows_in[0] = jnp.zeros(rows_in.shape[1:], jnp.float32)

    for side in range(2):
        column_copy(side).wait_recv()

    def spread_columns(k, _):
        for f in range(2):
            for half in range(2):
                spot = 4 * k + 2 * f + 64 * half
                west = pltpu.roll(cols_in[1], (126 - spot + LANES) % LANES, 1)
                east = pltpu.roll(cols_in[0], (LANES - spot) % LANES, 1)
                for t, x in ((0, west), (TILES + 1, east)):
                    for n, part in enumerate(split(x)):
                        parts[f, n, k, t, pl.ds(4 * half, 4)] = part.reshape(4, 16, LANES)
        return _

    lax.fori_loop(0, LEV, spread_columns, 0)

    @pl.when(lat > 0)
    def _():
        north.wait_recv()

    south.wait_recv()

    @pl.when(top_tile)
    def _():
        lanes = lax.broadcasted_iota(jnp.int32, (8, LANES), 1)

        def turn(pair, _):
            old = [rows_in[1, pair, t] for t in range(TILES)]
            for t in range(TILES):
                x = old[TILES - 1 - t]
                x = jnp.where(sub % 2 == 0, pltpu.roll(x, 7, 0), pltpu.roll(x, 1, 0))
                rows_in[1, pair, t] = -jnp.take_along_axis(x, LANES - 1 - lanes, axis=1)
            return _

        lax.fori_loop(0, LEV // 2, turn, 0)

    def spread_rows(pair, _):
        for t in range(TILES):
            for side, shifts, rows in ((0, (6, 4, 2, 0), 0), (1, (0, 6, 4, 2), ROWS // 8 + 1)):
                x = rows_in[side, pair, t]
                for n, s in enumerate(shifts):
                    buf = (ub, vb)[n % 2]
                    buf[2 * pair + n // 2, t, rows] = pltpu.roll(x, s, 0) if s else x
        return _

    lax.fori_loop(0, LEV // 2, spread_rows, 0)

    nearer = lax.broadcasted_iota(jnp.int32, (LEV * 16, LANES), 1) < 64

    def slope_x(f, c, b):
        total = None
        for n in range(PARTS):
            here, left, right = (parts[f, n, :, c + i, b].reshape(LEV * 16, LANES) for i in (1, 0, 2))
            cells = jnp.concatenate([here, jnp.where(nearer, right, left)], axis=1)
            term = jnp.dot(cells, band[...], preferred_element_type=jnp.float32)
            total = term if total is None else total + term
        return total.reshape(LEV, 2, 8, LANES)

    def slope_y(buf, k, c, tile):
        here, near, far = (buf[k, c, tile + i] for i in (1, 0, 2))

        def at(s):
            if s < 0:
                return pltpu.roll(jnp.where(sub < 8 + s, here, near), -s, 0)
            return pltpu.roll(jnp.where(sub >= s, here, far), 8 - s, 0)

        return (at(-2) - at(2)) + 8.0 * (at(1) - at(-1))

    def slopes(j, slot):
        for f in range(2):
            dx[slot, f] = slope_x(f, plan_ref[j], plan_ref[COLUMNS + j])

    def solve(j, slot):
        c = plan_ref[j]
        b = plan_ref[COLUMNS + j]
        halves = []
        for h in range(2):
            tile = 2 * b + h
            depth = bottom[c, tile]
            wide = scale[tile]
            wide4 = 4.0 * wide
            state = []
            for k in range(LEV):
                ux, vx = dx[slot, 0, k, h], dx[slot, 1, k, h]
                uy, vy = slope_y(ub, k, c, tile), slope_y(vb, k, c, tile)
                strain = ux * wide - vy
                okubo = strain * strain + (vx * wide4) * uy
                value = okubo * jnp.where(depth > k, coef[k], 0.0)
                if k > 0:
                    value = value + coef[LEV + k] * state[k - 1]
                state.append(value)
            for k in range(LEV - 2, -1, -1):
                state[k] = state[k] + coef[2 * LEV + k] * state[k + 1]
            halves.append(state)
        for k in range(LEV):
            both = jnp.concatenate([halves[0][k], halves[1][k]], axis=0)
            bricks[k // 4 * COLUMNS + j, k % 4] = both.astype(jnp.bfloat16)

    def send(step):
        to_lon, to_lat = target(lon, lat, step + 1)
        outbox[step] = bricks[plan_ref[2 * COLUMNS + step]]
        pltpu.make_async_remote_copy(
            outbox.at[step], out_ref.at[me], send_sem, recv_sem,
            device_id=(to_lon, to_lat), device_id_type=MESH,
        ).start()

    slopes(0, 0)
    pl.semaphore_wait(ready, N_LON - 1)

    def two(n, _):
        j = 2 * n
        slopes(j + 1, 1)
        solve(j, 0)
        send(j)
        slopes(lax.rem(j + 2, COLUMNS), 0)
        solve(j + 1, 1)
        send(j + 1)
        return _

    lax.fori_loop(0, COLUMNS // 2, two, 0)

    def rest(step, _):
        send(step)
        return _

    lax.fori_loop(COLUMNS, DEVICES - 1, rest, 0)
    out_ref[me] = bricks[plan_ref[2 * COLUMNS + DEVICES - 1]]

    column_copy(0).wait_send()
    column_copy(1).wait_send()
    north.wait_send()

    @pl.when(lat > 0)
    def _():
        south.wait_send()

    whole = pltpu.make_async_remote_copy(
        outbox.at[pl.ds(0, DEVICES - 1)], out_ref.at[pl.ds(0, DEVICES - 1)], send_sem, recv_sem,
        device_id=(lon, lat), device_id_type=MESH,
    )
    whole.wait_send()
    whole.wait_recv()


def by_tile(x):
    return x.reshape(*x.shape[:-2], x.shape[-2] // 8, 8, x.shape[-1])


def body(u_velocity, v_velocity, bottom_level, zonal_scale, mixing, brick_owner):
    brick = (DEVICES, 4, 16, LANES)
    dma = pltpu.SemaphoreType.DMA
    vmem, smem, hbm = (
        pl.BlockSpec(memory_space=pltpu.VMEM),
        pl.BlockSpec(memory_space=pltpu.SMEM),
        pl.BlockSpec(memory_space=pltpu.HBM),
    )
    out = pl.pallas_call(
        kernel,
        out_shape=pltpu.VMEM(brick, jnp.bfloat16),
        in_specs=[hbm, hbm, hbm, vmem, smem, smem],
        out_specs=vmem,
        scratch_shapes=[
            pltpu.VMEM((LEV, TILES, ROWS // 8 + 2, 8, LANES), jnp.float32),
            pltpu.VMEM((LEV, TILES, ROWS // 8 + 2, 8, LANES), jnp.float32),
            pltpu.VMEM((2, PARTS, LEV, TILES + 2, ROWS // 16, 16, LANES), jnp.bfloat16),
            pltpu.VMEM((2 * LANES, LANES), jnp.bfloat16),
            pltpu.VMEM((2, 2, LEV, 2, 8, LANES), jnp.float32),
            pltpu.VMEM((TILES, ROWS // 8, 8, LANES), jnp.int32),
            pltpu.VMEM((ROWS // 8, 8, LANES), jnp.float32),
            pltpu.VMEM((3 * LEV, 8, LANES), jnp.float32),
            pltpu.VMEM(brick, jnp.bfloat16),
            pltpu.VMEM(brick, jnp.bfloat16),
            pltpu.VMEM((2, LEV // 2, TILES, 8, LANES), jnp.float32),
            pltpu.VMEM((2, LEV // 2, TILES, 8, LANES), jnp.float32),
            pltpu.VMEM((2, 64, LANES), jnp.float32),
            pltpu.VMEM((2, 64, LANES), jnp.float32),
            dma((LEV // GROUP, TILES, 2)),
            dma((TILES,)),
            dma((4,)),
            dma((4,)),
            dma,
            dma,
            dma,
            pltpu.SemaphoreType.REGULAR,
        ],
        compiler_params=pltpu.CompilerParams(
            collective_id=0, has_side_effects=True, vmem_limit_bytes=56 << 20
        ),
    )(by_tile(u_velocity), by_tile(v_velocity), by_tile(bottom_level), zonal_scale[None], mixing, plan(brick_owner))
    return out[None]


def solution(mesh):
    placed = (P(None, "lat", "lon"), P(None, "lat", "lon"), P("lat", "lon"), P("lat"), P(), P())
    return jax.shard_map(
        body,
        mesh=mesh,
        in_specs=placed,
        out_specs=P(("lon", "lat"), None, None, None, None),
        check_vma=False,
    )
```

```python
import jax
import jax.numpy as jnp
from jax import lax
from jax.experimental import pallas as pl
from jax.experimental.pallas import tpu as pltpu
from jax.sharding import PartitionSpec as P

MESH = pl.DeviceIdType.MESH
LEV, ROWS, TILES, LANES = 16, 128, 4, 128
N_LON, N_LAT = 8, 16
DEVICES = N_LON * N_LAT
COLUMNS = 32
PARTS = 3

GROUP = 4

def target(lon, lat, step):
    off = (step * 101) & (DEVICES - 1)
    x = (((lat >> 1 & 1) << 1) + (lon >> 2) + off) & 3
    y = (lon + (off >> 2)) & 3
    z = ((lat >> 2) + (off >> 4)) & 3
    core = (lat + (off >> 6)) & 1
    return ((x & 1) << 2) + y, (z << 2) + (x >> 1 << 1) + core

def plan(brick_owner):
    lon, lat = lax.axis_index("lon"), lax.axis_index("lat")
    steps = jnp.arange(DEVICES, dtype=jnp.int32)
    to_lon, to_lat = target(lon, lat, steps + 1)
    dest = to_lon * N_LAT + to_lat
    place = jnp.sum(jnp.where(brick_owner[None, :] == dest[:, None], steps[None, :], 0), axis=1)
    column = place % COLUMNS
    columns = jnp.arange(COLUMNS, dtype=jnp.int32)
    hit = column[None, :] == columns[:, None]
    need = jnp.min(jnp.where(hit, steps[None, :], DEVICES), axis=1)
    slot = jnp.sum((need[None, :] < need[:, None]).astype(jnp.int32), axis=1)
    order = jnp.sum(jnp.where(slot[None, :] == columns[:, None], columns[None, :], 0), axis=1)
    source = place // COLUMNS * COLUMNS + jnp.sum(jnp.where(hit, slot[:, None], 0), axis=0)
    return jnp.concatenate([order % TILES, order // TILES, source])

def split(x):
    parts = []
    for _ in range(PARTS - 1):
        part = x.astype(jnp.bfloat16)
        parts.append(part)
        x = x - part.astype(jnp.float32)
    return (*parts, x.astype(jnp.bfloat16))

def band_matrix(edges):
    shape = (2 * LANES, 2 * LANES)
    source = lax.broadcasted_iota(jnp.int32, shape, 0)
    to = lax.broadcasted_iota(jnp.int32, shape, 1)
    if edges:
        same = (source < LANES) == (to < LANES)
        cell, to = source % LANES, to % LANES
        source = jnp.where(same, jnp.where(cell < LANES // 2, cell + LANES, cell - LANES), 4 * LANES)
    gap = source - to
    weight = jnp.zeros(shape, jnp.float32)
    for at, w in ((-2, 1.0), (-1, -8.0), (1, 8.0), (2, -1.0)):
        weight = jnp.where(gap == at, w, weight)
    return weight.astype(jnp.bfloat16)

def kernel(
    u_hbm, v_hbm, bottom_hbm, scale_ref, mixing_ref, plan_ref, out_ref,
    ub, vb, parts, edges, band, dx, bottom, scale, coef, bricks, outbox, rows_out, rows_in, cols_out, cols_in,
    load_sem, bottom_sem, halo_send, halo_recv, own_sem, send_sem, recv_sem, ready,
):
    lon, lat = lax.axis_index("lon"), lax.axis_index("lat")
    me = lon * N_LAT + lat
    barrier = pltpu.get_barrier_semaphore()

    def signal(sem, to):
        pl.semaphore_signal(sem, inc=1, device_id=to, device_id_type=MESH)

    for k in range(1, N_LAT):
        signal(barrier, (lon, (lat + k) % N_LAT))
    for k in range(1, N_LON):
        signal(barrier, ((lon + k) % N_LON, lat))

    loads = []
    for t in range(TILES):
        cut = pl.ds(t * LANES, LANES)
        c = pltpu.make_async_copy(bottom_hbm.at[:, :, cut], bottom.at[t], bottom_sem.at[t])
        c.start()
        loads.append(c)
    for g in range(LEV // GROUP):
        for t in range(TILES):
            cut = pl.ds(t * LANES, LANES)
            levels = pl.ds(g * GROUP, GROUP)
            for f, (src, dst) in enumerate(((u_hbm, ub), (v_hbm, vb))):
                c = pltpu.make_async_copy(
                    src.at[levels, :, :, cut],
                    dst.at[levels, t, pl.ds(1, ROWS // 8)],
                    load_sem.at[g, t, f],
                )
                c.start()
                loads.append(c)

    scale[...] = jnp.broadcast_to(scale_ref[...], (ROWS, LANES)).T.reshape(ROWS // 8, 8, LANES)
    band[0] = band_matrix(False)
    band[1] = band_matrix(True)
    one = jnp.ones((8, LANES), jnp.float32)
    ratio = None
    for k in range(LEV):
        above = mixing_ref[k - 1] * one if k > 0 else None
        below = mixing_ref[k] * one if k < LEV - 1 else None
        pivot = one
        if k > 0:
            pivot = pivot + above
        if k < LEV - 1:
            pivot = pivot + below
        if k > 0:
            pivot = pivot - above * ratio
        inverse = 1.0 / pivot
        coef[k] = inverse * (1.0 / 144.0)
        if k > 0:
            coef[LEV + k] = above * inverse
        if k < LEV - 1:
            ratio = below * inverse
            coef[2 * LEV + k] = ratio

    sub = lax.broadcasted_iota(jnp.int32, (8, LANES), 0)
    lane = lax.broadcasted_iota(jnp.int32, (64, LANES), 1)

    for c in loads[:TILES]:
        c.wait()
    nearer = lax.broadcasted_iota(jnp.int32, (ROWS, LANES), 1) < 64

    def slopes(g):
        levels = pl.ds(g * GROUP, GROUP)
        shape = (GROUP, ROWS // 8, 8, LANES)

        def product(cells, which):
            total = None
            for p in range(PARTS):
                lhs = cells(p).reshape(GROUP * ROWS, 2 * LANES)
                term = jnp.dot(lhs, band[which], preferred_element_type=jnp.float32)
                total = term if total is None else total + term
            return total

        across = product(lambda p: edges[p, levels], 1)
        for f in range(2):
            add = across[:, f * LANES : (f + 1) * LANES].reshape(GROUP, ROWS, LANES)
            for pair in range(2):
                total = product(lambda p: parts[f, p, pair, levels], 0)
                for i in range(2):
                    x = total[:, i * LANES : (i + 1) * LANES].reshape(GROUP, ROWS, LANES)
                    if pair == 0 and i == 1:
                        x = x + jnp.where(nearer, 0.0, add)
                    if pair == 1 and i == 0:
                        x = x + jnp.where(nearer, add, 0.0)
                    dx[f, levels, 2 * pair + i] = x.reshape(shape)

    west = jnp.zeros((64, LANES), jnp.float32)
    east = jnp.zeros((64, LANES), jnp.float32)
    for g in range(LEV // GROUP):
        for c in loads[TILES + g * 2 * TILES : TILES + (g + 1) * 2 * TILES]:
            c.wait()

        def mask_pair(n, carry):
            west, east = carry
            for j in range(2):
                k = g * GROUP + 2 * n + j
                seas = [bottom[t] > k for t in range(TILES)]
                for f, buf in enumerate((ub, vb)):
                    split_tiles = []
                    for t in range(TILES):
                        now = jnp.where(seas[t], buf[k, t, pl.ds(1, ROWS // 8)], 0.0)
                        buf[k, t, pl.ds(1, ROWS // 8)] = now
                        split_tiles.append(split(now.reshape(ROWS, LANES)))
                        for p in range(PARTS):
                            parts[f, p, t // 2, k, :, pl.ds(t % 2 * LANES, LANES)] = split_tiles[t][p]
                    for p in range(PARTS):
                        edges[p, k, :, pl.ds(f * LANES, LANES)] = jnp.where(
                            nearer, split_tiles[2][p], split_tiles[1][p]
                        )
                for f, buf in enumerate((ub, vb)):
                    at = 4 * k + 2 * f
                    for half in range(2):
                        first = buf[k, 0, pl.ds(1 + 8 * half, 8)].reshape(64, LANES)
                        last = buf[k, TILES - 1, pl.ds(1 + 8 * half, 8)].reshape(64, LANES)
                        spot = at + 64 * half
                        here = (lane >= spot) & (lane < spot + 2)
                        west = jnp.where(here, pltpu.roll(first, spot, 1), west)
                        east = jnp.where(here, pltpu.roll(last, (spot + 2) % LANES, 1), east)
            k = g * GROUP + 2 * n
            pair = k // 2
            for t in range(TILES):
                top = [b[k + j, t, ROWS // 8] for j in range(2) for b in (ub, vb)]
                low = [b[k + j, t, 1] for j in range(2) for b in (ub, vb)]
                top = [pltpu.roll(x, s, 0) if s else x for x, s in zip(top, (2, 4, 6, 0))]
                low = [pltpu.roll(x, s, 0) if s else x for x, s in zip(low, (0, 2, 4, 6))]
                for side, q in ((0, top), (1, low)):
                    rows_out[side, pair, t] = jnp.where(
                        sub < 4, jnp.where(sub < 2, q[0], q[1]), jnp.where(sub < 6, q[2], q[3])
                    )
            return west, east

        west, east = lax.fori_loop(0, GROUP // 2, mask_pair, (west, east))

    cols_out[0] = west
    cols_out[1] = east

    pl.semaphore_wait(barrier, N_LAT - 1 + N_LON - 1)
    for k in range(1, N_LON):
        signal(ready, ((lon + k) % N_LON, lat))

    def column_copy(side):
        to = (lon + (N_LON - 1 if side == 0 else 1)) % N_LON
        return pltpu.make_async_remote_copy(
            cols_out.at[side], cols_in.at[side], halo_send.at[side], halo_recv.at[side],
            device_id=(to, lat), device_id_type=MESH,
        )

    def row_copy(src, dst, sem, to):
        return pltpu.make_async_remote_copy(
            rows_out.at[src], rows_in.at[dst], halo_send.at[sem], halo_recv.at[2 + dst],
            device_id=to, device_id_type=MESH,
        )

    top_tile = lat == N_LAT - 1
    north = row_copy(0, 0, 2, (lon, (lat + 1) % N_LAT))
    fold = row_copy(0, 1, 2, (N_LON - 1 - lon, lat))
    south = row_copy(1, 1, 3, (lon, (lat + N_LAT - 1) % N_LAT))

    @pl.when(top_tile)
    def _():
        fold.start()

    @pl.when(jnp.logical_not(top_tile))
    def _():
        north.start()

    @pl.when(lat > 0)
    def _():
        south.start()

    for side in range(2):
        column_copy(side).start()

    @pl.when(lat == 0)
    def _():
        rows_in[0] = jnp.zeros(rows_in.shape[1:], jnp.float32)

    for g in range(LEV // GROUP):
        slopes(g)

    for side in range(2):
        column_copy(side).wait_recv()

    even = lane % 2 == 0
    cells = cols_in[1]
    cols_in[1] = jnp.where(even, cells - 8.0 * pltpu.roll(cells, LANES - 1, 1), cells)
    cells = cols_in[0]
    cols_in[0] = jnp.where(even, -cells, 8.0 * pltpu.roll(cells, 1, 1) - cells)

    def spread_columns(k, _):
        for f in range(2):
            for half in range(2):
                spot = 4 * k + 2 * f + 64 * half
                west = pltpu.roll(cols_in[1], (LANES - spot) % LANES, 1)
                east = pltpu.roll(cols_in[0], (126 - spot + LANES) % LANES, 1)
                west = jnp.where(lane < 2, west, 0.0).reshape(8, 8, LANES)
                east = jnp.where(lane >= 126, east, 0.0).reshape(8, 8, LANES)
                tiles = pl.ds(8 * half, 8)
                dx[f, k, 0, tiles] = dx[f, k, 0, tiles] + west
                dx[f, k, TILES - 1, tiles] = dx[f, k, TILES - 1, tiles] + east
        return _

    lax.fori_loop(0, LEV, spread_columns, 0)

    @pl.when(lat > 0)
    def _():
        north.wait_recv()

    south.wait_recv()

    @pl.when(top_tile)
    def _():
        lanes = lax.broadcasted_iota(jnp.int32, (8, LANES), 1)

        def turn(pair, _):
            old = [rows_in[1, pair, t] for t in range(TILES)]
            for t in range(TILES):
                x = old[TILES - 1 - t]
                x = jnp.where(sub % 2 == 0, pltpu.roll(x, 7, 0), pltpu.roll(x, 1, 0))
                rows_in[1, pair, t] = -jnp.take_along_axis(x, LANES - 1 - lanes, axis=1)
            return _

        lax.fori_loop(0, LEV // 2, turn, 0)

    def spread_rows(pair, _):
        for t in range(TILES):
            for side, shifts, rows in ((0, (6, 4, 2, 0), 0), (1, (0, 6, 4, 2), ROWS // 8 + 1)):
                x = rows_in[side, pair, t]
                for n, s in enumerate(shifts):
                    buf = (ub, vb)[n % 2]
                    buf[2 * pair + n // 2, t, rows] = pltpu.roll(x, s, 0) if s else x
        return _

    lax.fori_loop(0, LEV // 2, spread_rows, 0)

    def slope_y(buf, k, c, tile):
        here, near, far = (buf[k, c, tile + i] for i in (1, 0, 2))

        def at(s):
            if s < 0:
                return pltpu.roll(jnp.where(sub < 8 + s, here, near), -s, 0)
            return pltpu.roll(jnp.where(sub >= s, here, far), 8 - s, 0)

        return (at(-2) - at(2)) + 8.0 * (at(1) - at(-1))

    def solve(j):
        c = plan_ref[j]
        b = plan_ref[COLUMNS + j]
        halves = []
        for h in range(2):
            tile = 2 * b + h
            depth = bottom[c, tile]
            wide = scale[tile]
            wide4 = 4.0 * wide
            state = []
            for k in range(LEV):
                ux, vx = dx[0, k, c, tile], dx[1, k, c, tile]
                uy, vy = slope_y(ub, k, c, tile), slope_y(vb, k, c, tile)
                strain = ux * wide - vy
                okubo = strain * strain + (vx * wide4) * uy
                value = okubo * jnp.where(depth > k, coef[k], 0.0)
                if k > 0:
                    value = value + coef[LEV + k] * state[k - 1]
                state.append(value)
            for k in range(LEV - 2, -1, -1):
                state[k] = state[k] + coef[2 * LEV + k] * state[k + 1]
            halves.append(state)
        for k in range(LEV):
            both = jnp.concatenate([halves[0][k], halves[1][k]], axis=0)
            bricks[k // 4 * COLUMNS + j, k % 4] = both.astype(jnp.bfloat16)

    def send(step):
        to_lon, to_lat = target(lon, lat, step + 1)
        outbox[step] = bricks[plan_ref[2 * COLUMNS + step]]
        pltpu.make_async_remote_copy(
            outbox.at[step], out_ref.at[me], send_sem, recv_sem,
            device_id=(to_lon, to_lat), device_id_type=MESH,
        ).start()

    solve(0)
    pl.semaphore_wait(ready, N_LON - 1)

    def both(j, _):
        send(j - 1)
        solve(j)
        return _

    lax.fori_loop(1, COLUMNS, both, 0)

    def rest(step, _):
        send(step)
        return _

    lax.fori_loop(COLUMNS - 1, DEVICES - 1, rest, 0)
    out_ref[me] = bricks[plan_ref[2 * COLUMNS + DEVICES - 1]]

    column_copy(0).wait_send()
    column_copy(1).wait_send()
    north.wait_send()

    @pl.when(lat > 0)
    def _():
        south.wait_send()

    whole = pltpu.make_async_remote_copy(
        outbox.at[pl.ds(0, DEVICES - 1)], out_ref.at[pl.ds(0, DEVICES - 1)], send_sem, recv_sem,
        device_id=(lon, lat), device_id_type=MESH,
    )
    whole.wait_send()
    whole.wait_recv()

def by_tile(x):
    return x.reshape(*x.shape[:-2], x.shape[-2] // 8, 8, x.shape[-1])

def body(u_velocity, v_velocity, bottom_level, zonal_scale, mixing, brick_owner):
    brick = (DEVICES, 4, 16, LANES)
    dma = pltpu.SemaphoreType.DMA
    vmem, smem, hbm = (
        pl.BlockSpec(memory_space=pltpu.VMEM),
        pl.BlockSpec(memory_space=pltpu.SMEM),
        pl.BlockSpec(memory_space=pltpu.HBM),
    )
    out = pl.pallas_call(
        kernel,
        out_shape=pltpu.VMEM(brick, jnp.bfloat16),
        in_specs=[hbm, hbm, hbm, vmem, smem, smem],
        out_specs=vmem,
        scratch_shapes=[
            pltpu.VMEM((LEV, TILES, ROWS // 8 + 2, 8, LANES), jnp.float32),
            pltpu.VMEM((LEV, TILES, ROWS // 8 + 2, 8, LANES), jnp.float32),
            pltpu.VMEM((2, PARTS, TILES // 2, LEV, ROWS, 2 * LANES), jnp.bfloat16),
            pltpu.VMEM((PARTS, LEV, ROWS, 2 * LANES), jnp.bfloat16),
            pltpu.VMEM((2, 2 * LANES, 2 * LANES), jnp.bfloat16),
            pltpu.VMEM((2, LEV, TILES, ROWS // 8, 8, LANES), jnp.float32),
            pltpu.VMEM((TILES, ROWS // 8, 8, LANES), jnp.int32),
            pltpu.VMEM((ROWS // 8, 8, LANES), jnp.float32),
            pltpu.VMEM((3 * LEV, 8, LANES), jnp.float32),
            pltpu.VMEM(brick, jnp.bfloat16),
            pltpu.VMEM(brick, jnp.bfloat16),
            pltpu.VMEM((2, LEV // 2, TILES, 8, LANES), jnp.float32),
            pltpu.VMEM((2, LEV // 2, TILES, 8, LANES), jnp.float32),
            pltpu.VMEM((2, 64, LANES), jnp.float32),
            pltpu.VMEM((2, 64, LANES), jnp.float32),
            dma((LEV // GROUP, TILES, 2)),
            dma((TILES,)),
            dma((4,)),
            dma((4,)),
            dma,
            dma,
            dma,
            pltpu.SemaphoreType.REGULAR,
        ],
        compiler_params=pltpu.CompilerParams(
            collective_id=0, has_side_effects=True, vmem_limit_bytes=56 << 20
        ),
    )(by_tile(u_velocity), by_tile(v_velocity), by_tile(bottom_level), zonal_scale[None], mixing, plan(brick_owner))
    return out[None]

def solution(mesh):
    placed = (P(None, "lat", "lon"), P(None, "lat", "lon"), P("lat", "lon"), P("lat"), P(), P())
    return jax.shard_map(
        body,
        mesh=mesh,
        in_specs=placed,
        out_specs=P(("lon", "lat"), None, None, None, None),
        check_vma=False,
    )
```

```python
import jax
import jax.numpy as jnp
from jax import lax
from jax.experimental import pallas as pl
from jax.experimental.pallas import tpu as pltpu
from jax.sharding import PartitionSpec as P

MESH = pl.DeviceIdType.MESH
LEV, ROWS, TILES, LANES = 16, 128, 4, 128
N_LON, N_LAT = 8, 16
DEVICES = N_LON * N_LAT
COLUMNS = 32
PARTS = 3

GROUP = 4

def target(lon, lat, step):
    off = (step * 101) & (DEVICES - 1)
    x = (((lat >> 1 & 1) << 1) + (lon >> 2) + off) & 3
    y = (lon + (off >> 2)) & 3
    z = ((lat >> 2) + (off >> 4)) & 3
    core = (lat + (off >> 6)) & 1
    return ((x & 1) << 2) + y, (z << 2) + (x >> 1 << 1) + core

def plan(owner, lon, lat):
    shape = (DEVICES, DEVICES)
    down = lax.broadcasted_iota(jnp.int32, shape, 0)
    along = lax.broadcasted_iota(jnp.int32, shape, 1)

    def total(x, axis):
        return jnp.broadcast_to(jnp.sum(x.astype(jnp.float32), axis=axis, keepdims=True), shape)

    to_lon, to_lat = target(lon, lat, down + 1)
    place = total(jnp.where(owner == to_lon * N_LAT + to_lat, along, 0), 1).astype(jnp.int32)
    place = place & (DEVICES - 1)
    hit = (place & (COLUMNS - 1)) == along
    need = jnp.broadcast_to(
        jnp.min(jnp.where(hit, down, DEVICES).astype(jnp.float32), axis=0, keepdims=True), shape
    )
    slot = total(jnp.where(need.T < need, 1, 0), 0)
    order = total(jnp.where(slot.astype(jnp.int32) == down, jnp.where(along < COLUMNS, along, 0), 0), 1)
    source = total(jnp.where(hit, slot, 0.0), 1) + (place - (place & (COLUMNS - 1))).astype(jnp.float32)
    order, source = order.T[:8].astype(jnp.int32), source.T[:8].astype(jnp.int32)
    order, source = order & (COLUMNS - 1), source & (DEVICES - 1)
    row = down[:8]
    return jnp.where(row == 0, order & (TILES - 1), jnp.where(row == 1, order >> 2, source))


def split(x):
    parts = []
    for _ in range(PARTS - 1):
        part = x.astype(jnp.bfloat16)
        parts.append(part)
        x = x - part.astype(jnp.float32)
    return (*parts, x.astype(jnp.bfloat16))

def band_matrix(edges):
    shape = (2 * LANES, 2 * LANES)
    source = lax.broadcasted_iota(jnp.int32, shape, 0)
    to = lax.broadcasted_iota(jnp.int32, shape, 1)
    if edges:
        same = (source < LANES) == (to < LANES)
        cell, to = source % LANES, to % LANES
        source = jnp.where(same, jnp.where(cell < LANES // 2, cell + LANES, cell - LANES), 4 * LANES)
    gap = source - to
    weight = jnp.zeros(shape, jnp.float32)
    for at, w in ((-2, 1.0), (-1, -8.0), (1, 8.0), (2, -1.0)):
        weight = jnp.where(gap == at, w, weight)
    return weight.astype(jnp.bfloat16)

def kernel(
    u_hbm, v_hbm, bottom_hbm, scale_ref, mixing_ref, owner_ref, out_ref,
    ub, vb, parts, edges, band, dx, bottom, scale, coef, bricks, outbox, rows_out, rows_in, cols_out, cols_in,
    plan_made, plan_ref, plan_sem, load_sem, bottom_sem, halo_send, halo_recv, own_sem, send_sem, recv_sem, ready,
):
    lon, lat = lax.axis_index("lon"), lax.axis_index("lat")
    me = lon * N_LAT + lat
    barrier = pltpu.get_barrier_semaphore()

    def signal(sem, to):
        pl.semaphore_signal(sem, inc=1, device_id=to, device_id_type=MESH)

    for k in range(1, N_LAT):
        signal(barrier, (lon, (lat + k) % N_LAT))
    for k in range(1, N_LON):
        signal(barrier, ((lon + k) % N_LON, lat))

    loads = []
    for t in range(TILES):
        cut = pl.ds(t * LANES, LANES)
        c = pltpu.make_async_copy(bottom_hbm.at[:, :, cut], bottom.at[t], bottom_sem.at[t])
        c.start()
        loads.append(c)
    for g in range(LEV // GROUP):
        for t in range(TILES):
            cut = pl.ds(t * LANES, LANES)
            levels = pl.ds(g * GROUP, GROUP)
            for f, (src, dst) in enumerate(((u_hbm, ub), (v_hbm, vb))):
                c = pltpu.make_async_copy(
                    src.at[levels, :, :, cut],
                    dst.at[levels, t, pl.ds(1, ROWS // 8)],
                    load_sem.at[g, t, f],
                )
                c.start()
                loads.append(c)

    plan_made[...] = plan(jnp.broadcast_to(owner_ref[...], (DEVICES, DEVICES)), lon, lat)
    plan_copy = pltpu.make_async_copy(plan_made, plan_ref, plan_sem)
    plan_copy.start()

    scale[...] = jnp.broadcast_to(scale_ref[...], (ROWS, LANES)).T.reshape(ROWS // 8, 8, LANES)
    band[0] = band_matrix(False)
    band[1] = band_matrix(True)
    one = jnp.ones((8, LANES), jnp.float32)
    ratio = None
    for k in range(LEV):
        above = mixing_ref[k - 1] * one if k > 0 else None
        below = mixing_ref[k] * one if k < LEV - 1 else None
        pivot = one
        if k > 0:
            pivot = pivot + above
        if k < LEV - 1:
            pivot = pivot + below
        if k > 0:
            pivot = pivot - above * ratio
        inverse = 1.0 / pivot
        coef[k] = inverse * (1.0 / 144.0)
        if k > 0:
            coef[LEV + k] = above * inverse
        if k < LEV - 1:
            ratio = below * inverse
            coef[2 * LEV + k] = ratio

    sub = lax.broadcasted_iota(jnp.int32, (8, LANES), 0)
    lane = lax.broadcasted_iota(jnp.int32, (64, LANES), 1)

    for c in loads[:TILES]:
        c.wait()
    nearer = lax.broadcasted_iota(jnp.int32, (ROWS, LANES), 1) < 64

    def slopes(g):
        levels = pl.ds(g * GROUP, GROUP)
        shape = (GROUP, ROWS // 8, 8, LANES)

        def product(cells, which):
            total = None
            for p in range(PARTS):
                lhs = cells(p).reshape(GROUP * ROWS, 2 * LANES)
                term = jnp.dot(lhs, band[which], preferred_element_type=jnp.float32)
                total = term if total is None else total + term
            return total

        across = product(lambda p: edges[p, levels], 1)
        for f in range(2):
            add = across[:, f * LANES : (f + 1) * LANES].reshape(GROUP, ROWS, LANES)
            for pair in range(2):
                total = product(lambda p: parts[f, p, pair, levels], 0)
                for i in range(2):
                    x = total[:, i * LANES : (i + 1) * LANES].reshape(GROUP, ROWS, LANES)
                    if pair == 0 and i == 1:
                        x = x + jnp.where(nearer, 0.0, add)
                    if pair == 1 and i == 0:
                        x = x + jnp.where(nearer, add, 0.0)
                    dx[f, levels, 2 * pair + i] = x.reshape(shape)

    west = jnp.zeros((64, LANES), jnp.float32)
    east = jnp.zeros((64, LANES), jnp.float32)
    for g in range(LEV // GROUP):
        for c in loads[TILES + g * 2 * TILES : TILES + (g + 1) * 2 * TILES]:
            c.wait()

        def mask_pair(n, carry):
            west, east = carry
            for j in range(2):
                k = g * GROUP + 2 * n + j
                seas = [bottom[t] > k for t in range(TILES)]
                for f, buf in enumerate((ub, vb)):
                    split_tiles = []
                    for t in range(TILES):
                        now = jnp.where(seas[t], buf[k, t, pl.ds(1, ROWS // 8)], 0.0)
                        buf[k, t, pl.ds(1, ROWS // 8)] = now
                        split_tiles.append(split(now.reshape(ROWS, LANES)))
                        for p in range(PARTS):
                            parts[f, p, t // 2, k, :, pl.ds(t % 2 * LANES, LANES)] = split_tiles[t][p]
                    for p in range(PARTS):
                        edges[p, k, :, pl.ds(f * LANES, LANES)] = jnp.where(
                            nearer, split_tiles[2][p], split_tiles[1][p]
                        )
                for f, buf in enumerate((ub, vb)):
                    at = 4 * k + 2 * f
                    for half in range(2):
                        first = buf[k, 0, pl.ds(1 + 8 * half, 8)].reshape(64, LANES)
                        last = buf[k, TILES - 1, pl.ds(1 + 8 * half, 8)].reshape(64, LANES)
                        spot = at + 64 * half
                        here = (lane >= spot) & (lane < spot + 2)
                        west = jnp.where(here, pltpu.roll(first, spot, 1), west)
                        east = jnp.where(here, pltpu.roll(last, (spot + 2) % LANES, 1), east)
            k = g * GROUP + 2 * n
            pair = k // 2
            for t in range(TILES):
                top = [b[k + j, t, ROWS // 8] for j in range(2) for b in (ub, vb)]
                low = [b[k + j, t, 1] for j in range(2) for b in (ub, vb)]
                top = [pltpu.roll(x, s, 0) if s else x for x, s in zip(top, (2, 4, 6, 0))]
                low = [pltpu.roll(x, s, 0) if s else x for x, s in zip(low, (0, 2, 4, 6))]
                for side, q in ((0, top), (1, low)):
                    rows_out[side, pair, t] = jnp.where(
                        sub < 4, jnp.where(sub < 2, q[0], q[1]), jnp.where(sub < 6, q[2], q[3])
                    )
            return west, east

        west, east = lax.fori_loop(0, GROUP // 2, mask_pair, (west, east))

    cols_out[0] = west
    cols_out[1] = east

    pl.semaphore_wait(barrier, N_LAT - 1 + N_LON - 1)
    for k in range(1, N_LON):
        signal(ready, ((lon + k) % N_LON, lat))

    def column_copy(side):
        to = (lon + (N_LON - 1 if side == 0 else 1)) % N_LON
        return pltpu.make_async_remote_copy(
            cols_out.at[side], cols_in.at[side], halo_send.at[side], halo_recv.at[side],
            device_id=(to, lat), device_id_type=MESH,
        )

    def row_copy(src, dst, sem, to):
        return pltpu.make_async_remote_copy(
            rows_out.at[src], rows_in.at[dst], halo_send.at[sem], halo_recv.at[2 + dst],
            device_id=to, device_id_type=MESH,
        )

    top_tile = lat == N_LAT - 1
    north = row_copy(0, 0, 2, (lon, (lat + 1) % N_LAT))
    fold = row_copy(0, 1, 2, (N_LON - 1 - lon, lat))
    south = row_copy(1, 1, 3, (lon, (lat + N_LAT - 1) % N_LAT))

    @pl.when(top_tile)
    def _():
        fold.start()

    @pl.when(jnp.logical_not(top_tile))
    def _():
        north.start()

    @pl.when(lat > 0)
    def _():
        south.start()

    for side in range(2):
        column_copy(side).start()

    @pl.when(lat == 0)
    def _():
        rows_in[0] = jnp.zeros(rows_in.shape[1:], jnp.float32)

    for g in range(LEV // GROUP):
        slopes(g)

    for side in range(2):
        column_copy(side).wait_recv()

    even = lane % 2 == 0
    cells = cols_in[1]
    cols_in[1] = jnp.where(even, cells - 8.0 * pltpu.roll(cells, LANES - 1, 1), cells)
    cells = cols_in[0]
    cols_in[0] = jnp.where(even, -cells, 8.0 * pltpu.roll(cells, 1, 1) - cells)

    def spread_columns(k, _):
        for f in range(2):
            for half in range(2):
                spot = 4 * k + 2 * f + 64 * half
                west = pltpu.roll(cols_in[1], (LANES - spot) % LANES, 1)
                east = pltpu.roll(cols_in[0], (126 - spot + LANES) % LANES, 1)
                west = jnp.where(lane < 2, west, 0.0).reshape(8, 8, LANES)
                east = jnp.where(lane >= 126, east, 0.0).reshape(8, 8, LANES)
                tiles = pl.ds(8 * half, 8)
                dx[f, k, 0, tiles] = dx[f, k, 0, tiles] + west
                dx[f, k, TILES - 1, tiles] = dx[f, k, TILES - 1, tiles] + east
        return _

    lax.fori_loop(0, LEV, spread_columns, 0)

    @pl.when(lat > 0)
    def _():
        north.wait_recv()

    south.wait_recv()

    @pl.when(top_tile)
    def _():
        lanes = lax.broadcasted_iota(jnp.int32, (8, LANES), 1)

        def turn(pair, _):
            old = [rows_in[1, pair, t] for t in range(TILES)]
            for t in range(TILES):
                x = old[TILES - 1 - t]
                x = jnp.where(sub % 2 == 0, pltpu.roll(x, 7, 0), pltpu.roll(x, 1, 0))
                rows_in[1, pair, t] = -jnp.take_along_axis(x, LANES - 1 - lanes, axis=1)
            return _

        lax.fori_loop(0, LEV // 2, turn, 0)

    def spread_rows(pair, _):
        for t in range(TILES):
            for side, shifts, rows in ((0, (6, 4, 2, 0), 0), (1, (0, 6, 4, 2), ROWS // 8 + 1)):
                x = rows_in[side, pair, t]
                for n, s in enumerate(shifts):
                    buf = (ub, vb)[n % 2]
                    buf[2 * pair + n // 2, t, rows] = pltpu.roll(x, s, 0) if s else x
        return _

    lax.fori_loop(0, LEV // 2, spread_rows, 0)

    def slope_y(buf, k, c, tile):
        here, near, far = (buf[k, c, tile + i] for i in (1, 0, 2))

        def at(s):
            if s < 0:
                return pltpu.roll(jnp.where(sub < 8 + s, here, near), -s, 0)
            return pltpu.roll(jnp.where(sub >= s, here, far), 8 - s, 0)

        return (at(-2) - at(2)) + 8.0 * (at(1) - at(-1))

    def solve(j):
        c = plan_ref[0, j]
        b = plan_ref[1, j]
        halves = []
        for h in range(2):
            tile = 2 * b + h
            depth = bottom[c, tile]
            wide = scale[tile]
            wide4 = 4.0 * wide
            state = []
            for k in range(LEV):
                ux, vx = dx[0, k, c, tile], dx[1, k, c, tile]
                uy, vy = slope_y(ub, k, c, tile), slope_y(vb, k, c, tile)
                strain = ux * wide - vy
                okubo = strain * strain + (vx * wide4) * uy
                value = okubo * jnp.where(depth > k, coef[k], 0.0)
                if k > 0:
                    value = value + coef[LEV + k] * state[k - 1]
                state.append(value)
            for k in range(LEV - 2, -1, -1):
                state[k] = state[k] + coef[2 * LEV + k] * state[k + 1]
            halves.append(state)
        for k in range(LEV):
            both = jnp.concatenate([halves[0][k], halves[1][k]], axis=0)
            bricks[k // 4 * COLUMNS + j, k % 4] = both.astype(jnp.bfloat16)

    def send(step):
        to_lon, to_lat = target(lon, lat, step + 1)
        outbox[step] = bricks[plan_ref[2, step]]
        pltpu.make_async_remote_copy(
            outbox.at[step], out_ref.at[me], send_sem, recv_sem,
            device_id=(to_lon, to_lat), device_id_type=MESH,
        ).start()

    plan_copy.wait()
    solve(0)
    pl.semaphore_wait(ready, N_LON - 1)

    def both(j, _):
        send(j - 1)
        solve(j)
        return _

    lax.fori_loop(1, COLUMNS, both, 0)

    def rest(step, _):
        send(step)
        return _

    lax.fori_loop(COLUMNS - 1, DEVICES - 1, rest, 0)
    out_ref[me] = bricks[plan_ref[2, DEVICES - 1]]

    column_copy(0).wait_send()
    column_copy(1).wait_send()
    north.wait_send()

    @pl.when(lat > 0)
    def _():
        south.wait_send()

    whole = pltpu.make_async_remote_copy(
        outbox.at[pl.ds(0, DEVICES - 1)], out_ref.at[pl.ds(0, DEVICES - 1)], send_sem, recv_sem,
        device_id=(lon, lat), device_id_type=MESH,
    )
    whole.wait_send()
    whole.wait_recv()

def by_tile(x):
    return x.reshape(*x.shape[:-2], x.shape[-2] // 8, 8, x.shape[-1])

def body(u_velocity, v_velocity, bottom_level, zonal_scale, mixing, brick_owner):
    brick = (DEVICES, 4, 16, LANES)
    dma = pltpu.SemaphoreType.DMA
    vmem, smem, hbm = (
        pl.BlockSpec(memory_space=pltpu.VMEM),
        pl.BlockSpec(memory_space=pltpu.SMEM),
        pl.BlockSpec(memory_space=pltpu.HBM),
    )
    out = pl.pallas_call(
        kernel,
        out_shape=pltpu.VMEM(brick, jnp.bfloat16),
        in_specs=[hbm, hbm, hbm, vmem, smem, vmem],
        out_specs=vmem,
        scratch_shapes=[
            pltpu.VMEM((LEV, TILES, ROWS // 8 + 2, 8, LANES), jnp.float32),
            pltpu.VMEM((LEV, TILES, ROWS // 8 + 2, 8, LANES), jnp.float32),
            pltpu.VMEM((2, PARTS, TILES // 2, LEV, ROWS, 2 * LANES), jnp.bfloat16),
            pltpu.VMEM((PARTS, LEV, ROWS, 2 * LANES), jnp.bfloat16),
            pltpu.VMEM((2, 2 * LANES, 2 * LANES), jnp.bfloat16),
            pltpu.VMEM((2, LEV, TILES, ROWS // 8, 8, LANES), jnp.float32),
            pltpu.VMEM((TILES, ROWS // 8, 8, LANES), jnp.int32),
            pltpu.VMEM((ROWS // 8, 8, LANES), jnp.float32),
            pltpu.VMEM((3 * LEV, 8, LANES), jnp.float32),
            pltpu.VMEM(brick, jnp.bfloat16),
            pltpu.VMEM(brick, jnp.bfloat16),
            pltpu.VMEM((2, LEV // 2, TILES, 8, LANES), jnp.float32),
            pltpu.VMEM((2, LEV // 2, TILES, 8, LANES), jnp.float32),
            pltpu.VMEM((2, 64, LANES), jnp.float32),
            pltpu.VMEM((2, 64, LANES), jnp.float32),
            pltpu.VMEM((8, DEVICES), jnp.int32),
            pltpu.SMEM((8, DEVICES), jnp.int32),
            dma,
            dma((LEV // GROUP, TILES, 2)),
            dma((TILES,)),
            dma((4,)),
            dma((4,)),
            dma,
            dma,
            dma,
            pltpu.SemaphoreType.REGULAR,
        ],
        compiler_params=pltpu.CompilerParams(
            collective_id=0, has_side_effects=True, vmem_limit_bytes=56 << 20
        ),
    )(by_tile(u_velocity), by_tile(v_velocity), by_tile(bottom_level), zonal_scale[None], mixing, brick_owner[None])
    return out[None]

def solution(mesh):
    placed = (P(None, "lat", "lon"), P(None, "lat", "lon"), P("lat", "lon"), P("lat"), P(), P())
    return jax.shard_map(
        body,
        mesh=mesh,
        in_specs=placed,
        out_specs=P(("lon", "lat"), None, None, None, None),
        check_vma=False,
    )
```

```python
import jax
import jax.numpy as jnp
from jax import lax
from jax.experimental import pallas as pl
from jax.experimental.pallas import tpu as pltpu
from jax.sharding import PartitionSpec as P

MESH = pl.DeviceIdType.MESH
LEV, ROWS, TILES, LANES = 16, 128, 4, 128
N_LON, N_LAT = 8, 16
DEVICES = N_LON * N_LAT
COLUMNS = 32
PARTS = 3

GROUP = 4

def target(lon, lat, step):
    off = (step * 101) & (DEVICES - 1)
    x = (((lat >> 1 & 1) << 1) + (lon >> 2) + off) & 3
    y = (lon + (off >> 2)) & 3
    z = ((lat >> 2) + (off >> 4)) & 3
    core = (lat + (off >> 6)) & 1
    return ((x & 1) << 2) + y, (z << 2) + (x >> 1 << 1) + core

def plan(owner, lon, lat):
    shape = (DEVICES, DEVICES)
    down = lax.broadcasted_iota(jnp.int32, shape, 0)
    along = lax.broadcasted_iota(jnp.int32, shape, 1)

    def total(x, axis):
        return jnp.broadcast_to(jnp.sum(x.astype(jnp.float32), axis=axis, keepdims=True), shape)

    to_lon, to_lat = target(lon, lat, down + 1)
    place = total(jnp.where(owner == to_lon * N_LAT + to_lat, along, 0), 1).astype(jnp.int32)
    place = place & (DEVICES - 1)
    hit = (place & (COLUMNS - 1)) == along
    need = jnp.broadcast_to(
        jnp.min(jnp.where(hit, down, DEVICES).astype(jnp.float32), axis=0, keepdims=True), shape
    )
    slot = total(jnp.where(need.T < need, 1, 0), 0)
    order = total(jnp.where(slot.astype(jnp.int32) == down, jnp.where(along < COLUMNS, along, 0), 0), 1)
    source = total(jnp.where(hit, slot, 0.0), 1) + (place - (place & (COLUMNS - 1))).astype(jnp.float32)
    order, source = order.T[:8].astype(jnp.int32), source.T[:8].astype(jnp.int32)
    order, source = order & (COLUMNS - 1), source & (DEVICES - 1)
    row = down[:8]
    return jnp.where(row == 0, order & (TILES - 1), jnp.where(row == 1, order >> 2, source))


def split(x):
    parts = []
    for _ in range(PARTS - 1):
        part = x.astype(jnp.bfloat16)
        parts.append(part)
        x = x - part.astype(jnp.float32)
    return (*parts, x.astype(jnp.bfloat16))

def band_matrix(edges):
    shape = (2 * LANES, 2 * LANES)
    source = lax.broadcasted_iota(jnp.int32, shape, 0)
    to = lax.broadcasted_iota(jnp.int32, shape, 1)
    if edges:
        same = (source < LANES) == (to < LANES)
        cell, to = source % LANES, to % LANES
        source = jnp.where(same, jnp.where(cell < LANES // 2, cell + LANES, cell - LANES), 4 * LANES)
    gap = source - to
    weight = jnp.zeros(shape, jnp.float32)
    for at, w in ((-2, 1.0), (-1, -8.0), (1, 8.0), (2, -1.0)):
        weight = jnp.where(gap == at, w, weight)
    return weight.astype(jnp.bfloat16)

def kernel(
    u_hbm, v_hbm, bottom_hbm, scale_ref, mixing_ref, owner_ref, out_ref,
    ub, vb, parts, edges, band, dx, bottom, scale, coef, bricks, outbox, rows_out, rows_in, cols_out, cols_in,
    plan_made, plan_ref, plan_sem, load_sem, bottom_sem, halo_send, halo_recv, own_sem, send_sem, recv_sem, ready,
):
    lon, lat = lax.axis_index("lon"), lax.axis_index("lat")
    me = lon * N_LAT + lat
    barrier = pltpu.get_barrier_semaphore()

    def signal(sem, to):
        pl.semaphore_signal(sem, inc=1, device_id=to, device_id_type=MESH)

    loads = []
    for t in range(TILES):
        cut = pl.ds(t * LANES, LANES)
        c = pltpu.make_async_copy(bottom_hbm.at[:, :, cut], bottom.at[t], bottom_sem.at[t])
        c.start()
        loads.append(c)
    for g in range(LEV // GROUP):
        for t in range(TILES):
            cut = pl.ds(t * LANES, LANES)
            levels = pl.ds(g * GROUP, GROUP)
            for f, (src, dst) in enumerate(((u_hbm, ub), (v_hbm, vb))):
                c = pltpu.make_async_copy(
                    src.at[levels, :, :, cut],
                    dst.at[levels, t, pl.ds(1, ROWS // 8)],
                    load_sem.at[g, t, f],
                )
                c.start()
                loads.append(c)

    for k in range(1, N_LAT):
        signal(barrier, (lon, (lat + k) % N_LAT))
    for k in range(1, N_LON):
        signal(barrier, ((lon + k) % N_LON, lat))

    plan_made[...] = plan(jnp.broadcast_to(owner_ref[...], (DEVICES, DEVICES)), lon, lat)
    plan_copy = pltpu.make_async_copy(plan_made, plan_ref, plan_sem)
    plan_copy.start()

    scale[...] = jnp.broadcast_to(scale_ref[...], (ROWS, LANES)).T.reshape(ROWS // 8, 8, LANES)
    band[0] = band_matrix(False)
    band[1] = band_matrix(True)
    one = jnp.ones((8, LANES), jnp.float32)
    ratio = None
    for k in range(LEV):
        above = mixing_ref[k - 1] * one if k > 0 else None
        below = mixing_ref[k] * one if k < LEV - 1 else None
        pivot = one
        if k > 0:
            pivot = pivot + above
        if k < LEV - 1:
            pivot = pivot + below
        if k > 0:
            pivot = pivot - above * ratio
        inverse = 1.0 / pivot
        coef[k] = inverse * (1.0 / 144.0)
        if k > 0:
            coef[LEV + k] = above * inverse
        if k < LEV - 1:
            ratio = below * inverse
            coef[2 * LEV + k] = ratio

    sub = lax.broadcasted_iota(jnp.int32, (8, LANES), 0)
    lane = lax.broadcasted_iota(jnp.int32, (64, LANES), 1)

    for c in loads[:TILES]:
        c.wait()
    nearer = lax.broadcasted_iota(jnp.int32, (ROWS, LANES), 1) < 64

    def slopes(g):
        levels = pl.ds(g * GROUP, GROUP)
        shape = (GROUP, ROWS // 8, 8, LANES)

        def product(cells, which):
            total = None
            for p in range(PARTS):
                lhs = cells(p).reshape(GROUP * ROWS, 2 * LANES)
                term = jnp.dot(lhs, band[which], preferred_element_type=jnp.float32)
                total = term if total is None else total + term
            return total

        across = product(lambda p: edges[p, levels], 1)
        for f in range(2):
            add = across[:, f * LANES : (f + 1) * LANES].reshape(GROUP, ROWS, LANES)
            for pair in range(2):
                total = product(lambda p: parts[f, p, pair, levels], 0)
                for i in range(2):
                    x = total[:, i * LANES : (i + 1) * LANES].reshape(GROUP, ROWS, LANES)
                    if pair == 0 and i == 1:
                        x = x + jnp.where(nearer, 0.0, add)
                    if pair == 1 and i == 0:
                        x = x + jnp.where(nearer, add, 0.0)
                    dx[f, levels, 2 * pair + i] = x.reshape(shape)

    west = jnp.zeros((64, LANES), jnp.float32)
    east = jnp.zeros((64, LANES), jnp.float32)
    for g in range(LEV // GROUP):
        for c in loads[TILES + g * 2 * TILES : TILES + (g + 1) * 2 * TILES]:
            c.wait()

        def mask_pair(n, carry):
            west, east = carry
            for j in range(2):
                k = g * GROUP + 2 * n + j
                seas = [bottom[t] > k for t in range(TILES)]
                for f, buf in enumerate((ub, vb)):
                    split_tiles = []
                    for t in range(TILES):
                        now = jnp.where(seas[t], buf[k, t, pl.ds(1, ROWS // 8)], 0.0)
                        buf[k, t, pl.ds(1, ROWS // 8)] = now
                        split_tiles.append(split(now.reshape(ROWS, LANES)))
                        for p in range(PARTS):
                            parts[f, p, t // 2, k, :, pl.ds(t % 2 * LANES, LANES)] = split_tiles[t][p]
                    for p in range(PARTS):
                        edges[p, k, :, pl.ds(f * LANES, LANES)] = jnp.where(
                            nearer, split_tiles[2][p], split_tiles[1][p]
                        )
                for f, buf in enumerate((ub, vb)):
                    at = 4 * k + 2 * f
                    for half in range(2):
                        first = buf[k, 0, pl.ds(1 + 8 * half, 8)].reshape(64, LANES)
                        last = buf[k, TILES - 1, pl.ds(1 + 8 * half, 8)].reshape(64, LANES)
                        spot = at + 64 * half
                        here = (lane >= spot) & (lane < spot + 2)
                        west = jnp.where(here, pltpu.roll(first, spot, 1), west)
                        east = jnp.where(here, pltpu.roll(last, (spot + 2) % LANES, 1), east)
            k = g * GROUP + 2 * n
            pair = k // 2
            for t in range(TILES):
                top = [b[k + j, t, ROWS // 8] for j in range(2) for b in (ub, vb)]
                low = [b[k + j, t, 1] for j in range(2) for b in (ub, vb)]
                top = [pltpu.roll(x, s, 0) if s else x for x, s in zip(top, (2, 4, 6, 0))]
                low = [pltpu.roll(x, s, 0) if s else x for x, s in zip(low, (0, 2, 4, 6))]
                for side, q in ((0, top), (1, low)):
                    rows_out[side, pair, t] = jnp.where(
                        sub < 4, jnp.where(sub < 2, q[0], q[1]), jnp.where(sub < 6, q[2], q[3])
                    )
            return west, east

        west, east = lax.fori_loop(0, GROUP // 2, mask_pair, (west, east))

    cols_out[0] = west
    cols_out[1] = east

    pl.semaphore_wait(barrier, N_LAT - 1 + N_LON - 1)
    for k in range(1, N_LON):
        signal(ready, ((lon + k) % N_LON, lat))

    def column_copy(side):
        to = (lon + (N_LON - 1 if side == 0 else 1)) % N_LON
        return pltpu.make_async_remote_copy(
            cols_out.at[side], cols_in.at[side], halo_send.at[side], halo_recv.at[side],
            device_id=(to, lat), device_id_type=MESH,
        )

    def row_copy(src, dst, sem, to):
        return pltpu.make_async_remote_copy(
            rows_out.at[src], rows_in.at[dst], halo_send.at[sem], halo_recv.at[2 + dst],
            device_id=to, device_id_type=MESH,
        )

    top_tile = lat == N_LAT - 1
    north = row_copy(0, 0, 2, (lon, (lat + 1) % N_LAT))
    fold = row_copy(0, 1, 2, (N_LON - 1 - lon, lat))
    south = row_copy(1, 1, 3, (lon, (lat + N_LAT - 1) % N_LAT))

    @pl.when(top_tile)
    def _():
        fold.start()

    @pl.when(jnp.logical_not(top_tile))
    def _():
        north.start()

    @pl.when(lat > 0)
    def _():
        south.start()

    for side in range(2):
        column_copy(side).start()

    @pl.when(lat == 0)
    def _():
        rows_in[0] = jnp.zeros(rows_in.shape[1:], jnp.float32)

    for g in range(LEV // GROUP):
        slopes(g)

    for side in range(2):
        column_copy(side).wait_recv()

    even = lane % 2 == 0
    cells = cols_in[1]
    cols_in[1] = jnp.where(even, cells - 8.0 * pltpu.roll(cells, LANES - 1, 1), cells)
    cells = cols_in[0]
    cols_in[0] = jnp.where(even, -cells, 8.0 * pltpu.roll(cells, 1, 1) - cells)

    def spread_columns(k, _):
        for f in range(2):
            for half in range(2):
                spot = 4 * k + 2 * f + 64 * half
                west = pltpu.roll(cols_in[1], (LANES - spot) % LANES, 1)
                east = pltpu.roll(cols_in[0], (126 - spot + LANES) % LANES, 1)
                west = jnp.where(lane < 2, west, 0.0).reshape(8, 8, LANES)
                east = jnp.where(lane >= 126, east, 0.0).reshape(8, 8, LANES)
                tiles = pl.ds(8 * half, 8)
                dx[f, k, 0, tiles] = dx[f, k, 0, tiles] + west
                dx[f, k, TILES - 1, tiles] = dx[f, k, TILES - 1, tiles] + east
        return _

    lax.fori_loop(0, LEV, spread_columns, 0)

    @pl.when(lat > 0)
    def _():
        north.wait_recv()

    south.wait_recv()

    @pl.when(top_tile)
    def _():
        lanes = lax.broadcasted_iota(jnp.int32, (8, LANES), 1)

        def turn(pair, _):
            old = [rows_in[1, pair, t] for t in range(TILES)]
            for t in range(TILES):
                x = old[TILES - 1 - t]
                x = jnp.where(sub % 2 == 0, pltpu.roll(x, 7, 0), pltpu.roll(x, 1, 0))
                rows_in[1, pair, t] = -jnp.take_along_axis(x, LANES - 1 - lanes, axis=1)
            return _

        lax.fori_loop(0, LEV // 2, turn, 0)

    def spread_rows(pair, _):
        for t in range(TILES):
            for side, shifts, rows in ((0, (6, 4, 2, 0), 0), (1, (0, 6, 4, 2), ROWS // 8 + 1)):
                x = rows_in[side, pair, t]
                for n, s in enumerate(shifts):
                    buf = (ub, vb)[n % 2]
                    buf[2 * pair + n // 2, t, rows] = pltpu.roll(x, s, 0) if s else x
        return _

    lax.fori_loop(0, LEV // 2, spread_rows, 0)

    def slope_y(buf, k, c, tile):
        here, near, far = (buf[k, c, tile + i] for i in (1, 0, 2))

        def at(s):
            if s < 0:
                return pltpu.roll(jnp.where(sub < 8 + s, here, near), -s, 0)
            return pltpu.roll(jnp.where(sub >= s, here, far), 8 - s, 0)

        return (at(-2) - at(2)) + 8.0 * (at(1) - at(-1))

    def solve(j):
        c = plan_ref[0, j]
        b = plan_ref[1, j]
        halves = []
        for h in range(2):
            tile = 2 * b + h
            depth = bottom[c, tile]
            wide = scale[tile]
            wide4 = 4.0 * wide
            state = []
            for k in range(LEV):
                ux, vx = dx[0, k, c, tile], dx[1, k, c, tile]
                uy, vy = slope_y(ub, k, c, tile), slope_y(vb, k, c, tile)
                strain = ux * wide - vy
                okubo = strain * strain + (vx * wide4) * uy
                value = okubo * jnp.where(depth > k, coef[k], 0.0)
                if k > 0:
                    value = value + coef[LEV + k] * state[k - 1]
                state.append(value)
            for k in range(LEV - 2, -1, -1):
                state[k] = state[k] + coef[2 * LEV + k] * state[k + 1]
            halves.append(state)
        for k in range(LEV):
            both = jnp.concatenate([halves[0][k], halves[1][k]], axis=0)
            bricks[k // 4 * COLUMNS + j, k % 4] = both.astype(jnp.bfloat16)

    def send(step):
        to_lon, to_lat = target(lon, lat, step + 1)
        outbox[step] = bricks[plan_ref[2, step]]
        pltpu.make_async_remote_copy(
            outbox.at[step], out_ref.at[me], send_sem, recv_sem,
            device_id=(to_lon, to_lat), device_id_type=MESH,
        ).start()

    plan_copy.wait()
    solve(0)
    pl.semaphore_wait(ready, N_LON - 1)

    def both(j, _):
        send(j - 1)
        solve(j)
        return _

    lax.fori_loop(1, COLUMNS, both, 0)

    def rest(step, _):
        send(step)
        return _

    lax.fori_loop(COLUMNS - 1, DEVICES - 1, rest, 0)
    out_ref[me] = bricks[plan_ref[2, DEVICES - 1]]

    column_copy(0).wait_send()
    column_copy(1).wait_send()
    north.wait_send()

    @pl.when(lat > 0)
    def _():
        south.wait_send()

    whole = pltpu.make_async_remote_copy(
        outbox.at[pl.ds(0, DEVICES - 1)], out_ref.at[pl.ds(0, DEVICES - 1)], send_sem, recv_sem,
        device_id=(lon, lat), device_id_type=MESH,
    )
    whole.wait_send()
    whole.wait_recv()

def by_tile(x):
    return x.reshape(*x.shape[:-2], x.shape[-2] // 8, 8, x.shape[-1])

def body(u_velocity, v_velocity, bottom_level, zonal_scale, mixing, brick_owner):
    brick = (DEVICES, 4, 16, LANES)
    dma = pltpu.SemaphoreType.DMA
    vmem, smem, hbm = (
        pl.BlockSpec(memory_space=pltpu.VMEM),
        pl.BlockSpec(memory_space=pltpu.SMEM),
        pl.BlockSpec(memory_space=pltpu.HBM),
    )
    out = pl.pallas_call(
        kernel,
        out_shape=pltpu.VMEM(brick, jnp.bfloat16),
        in_specs=[hbm, hbm, hbm, vmem, smem, vmem],
        out_specs=vmem,
        scratch_shapes=[
            pltpu.VMEM((LEV, TILES, ROWS // 8 + 2, 8, LANES), jnp.float32),
            pltpu.VMEM((LEV, TILES, ROWS // 8 + 2, 8, LANES), jnp.float32),
            pltpu.VMEM((2, PARTS, TILES // 2, LEV, ROWS, 2 * LANES), jnp.bfloat16),
            pltpu.VMEM((PARTS, LEV, ROWS, 2 * LANES), jnp.bfloat16),
            pltpu.VMEM((2, 2 * LANES, 2 * LANES), jnp.bfloat16),
            pltpu.VMEM((2, LEV, TILES, ROWS // 8, 8, LANES), jnp.float32),
            pltpu.VMEM((TILES, ROWS // 8, 8, LANES), jnp.int32),
            pltpu.VMEM((ROWS // 8, 8, LANES), jnp.float32),
            pltpu.VMEM((3 * LEV, 8, LANES), jnp.float32),
            pltpu.VMEM(brick, jnp.bfloat16),
            pltpu.VMEM(brick, jnp.bfloat16),
            pltpu.VMEM((2, LEV // 2, TILES, 8, LANES), jnp.float32),
            pltpu.VMEM((2, LEV // 2, TILES, 8, LANES), jnp.float32),
            pltpu.VMEM((2, 64, LANES), jnp.float32),
            pltpu.VMEM((2, 64, LANES), jnp.float32),
            pltpu.VMEM((8, DEVICES), jnp.int32),
            pltpu.SMEM((8, DEVICES), jnp.int32),
            dma,
            dma((LEV // GROUP, TILES, 2)),
            dma((TILES,)),
            dma((4,)),
            dma((4,)),
            dma,
            dma,
            dma,
            pltpu.SemaphoreType.REGULAR,
        ],
        compiler_params=pltpu.CompilerParams(
            collective_id=0, has_side_effects=True, vmem_limit_bytes=56 << 20
        ),
    )(by_tile(u_velocity), by_tile(v_velocity), by_tile(bottom_level), zonal_scale[None], mixing, brick_owner[None])
    return out[None]

def solution(mesh):
    placed = (P(None, "lat", "lon"), P(None, "lat", "lon"), P("lat", "lon"), P("lat"), P(), P())
    return jax.shard_map(
        body,
        mesh=mesh,
        in_specs=placed,
        out_specs=P(("lon", "lat"), None, None, None, None),
        check_vma=False,
    )
```
